32 devices in a mesh: zslab: 4 (over y, x), blk: 8 (over z, core).
Axes of the slice: x: 2, y: 2, z: 4, core: 2. Of those that a mesh axis runs over, the one named last changes fastest.
Arguments:
- field: bfloat16 [64, 16, 16, 128], P('blk', None, 'zslab'), may hold values from -6 to 6
- fracture_mask: int32 [64, 16, 16], P('blk', None, 'zslab'), may hold values 0 or 1
- dilation: int32 [2, 3], replicated, may hold values from 1 to 2, as said below
- conv_weight: bfloat16 [2, 3456, 128], replicated, may hold values from -0.109375 to 0.109375
- embed_weight: bfloat16 [8, 2048, 1024], P('zslab', 'blk'), may hold values from -0.046875 to 0.046875
- qkv_weight: bfloat16 [3, 1024, 1024], P(None, 'blk', 'zslab'), may hold values from -3 to 3
- out_grad: bfloat16 [128, 1024], P('blk', 'zslab'), may hold values from -6 to 6
Outputs:
- field_grad: bfloat16 [64, 16, 16, 128], P('blk', None, 'zslab')
The draws below stay inside these ranges and needn't reach their ends.
Inputs may be any that keep to these rules, and one draw needn't show every extreme that they name: The dilation of each of the 2 layers along x, y and z; some entry is 1 and some entry is 2.
All inputs are finite; a program needn't handle non-finite values. No bound on the sum of `fracture_mask` on one device may be relied on, other than what follows from the above.
Results may differ from the reference program's by a relative error of at most 0.04.
Values may be sent and summed in bfloat16 or wider, within the bound.
A program may use at most 64 MiB of HBM per device.

```python
import jax
import jax.numpy as jnp
from jax import lax

C = 128
HEADS = 8
HD = 128
D = 1024
PX = 8
PY = 8
PZ = 2
FEAT = 16384
NY = 16
LAYERS = 2
DMAX = 2
NX = 64
NZ = 16
TOKENS = 128


def draw_dilation(key, part):
    entries = jax.random.randint(jax.random.fold_in(key, 11), (LAYERS * 3,), 1, 3).astype(jnp.int32)
    order = jax.random.permutation(jax.random.fold_in(key, 13), LAYERS * 3)
    positions = jnp.arange(LAYERS * 3)
    entries = jnp.where(positions == order[0], 2, entries)
    entries = jnp.where(positions == order[1], 1, entries)
    return entries.reshape(LAYERS, 3).astype(jnp.int32)


def draw_qkv_weight(key, part):
    entries = jax.random.normal(key, (3, D, D), jnp.float32) * D ** (-0.5)
    return jnp.clip(entries, -3.0, 3.0).astype(jnp.bfloat16)


def place_ends(values, key, least, largest):
    longest = values.shape.index(max(values.shape))
    spots = []
    for shift in (0, 1):
        where = [jax.random.randint(jax.random.fold_in(key, axis), (), 0, length) for axis, length in enumerate(values.shape)]
        where[longest] = (where[longest] + shift) % values.shape[longest]
        spots.append(tuple(where))
    return values.at[spots[0]].set(least).at[spots[1]].set(largest)


def steps_of(stream_key, extent, shards, smallest, top_value):
    def one(position, shards_of):
        steps = jax.random.uniform(jax.random.fold_in(jax.random.fold_in(stream_key, 6), position), (shards_of,), jnp.float32, smallest / len(shards), top_value / len(shards))
        return jnp.repeat(jnp.exp(steps), extent[position] // shards_of).reshape((-1,) + (1,) * (len(extent) - position - 1))

    level = one(*shards[0])
    for cut in shards[1:]:
        level = level * one(*cut)
    return level


def centred(rng, shape, scale, bound, cuts=(), kind=jnp.bfloat16):
    values = scale * jax.random.normal(rng, shape, jnp.float32)
    if cuts:
        values = values * steps_of(rng, shape, cuts, -0.22, 0.18)
    return jnp.clip(values, -bound, bound).astype(kind)


def setup_inputs(seed: int = 0) -> dict:
    key_of = jax.random.split(jax.random.key(seed), 8)
    field = centred(key_of[0], (NX, NY, NZ, C), 1.0, 6.0, ((0, 8), (2, 4)))
    fracture_mask = place_ends((jax.random.randint(key_of[1], (NX, NY, NZ), 0, 3) < 1).astype(jnp.int32), jax.random.fold_in(key_of[1], 1), 0, 1)
    dilation = draw_dilation(jax.random.fold_in(key_of[7], 71), 0)
    conv_weight = centred(key_of[3], (LAYERS, 27 * C, C), (27 * C) ** -0.5, 0.109375)
    embed_weight = centred(key_of[4], (PX, PY * PZ * C, D), FEAT ** -0.5, 0.046875, ((0, 4), (1, 8)))
    qkv_weight = draw_qkv_weight(jax.random.fold_in(key_of[7], 71), 0)
    out_grad = centred(key_of[6], (TOKENS, D), 1.0, 6.0, ((0, 8), (1, 4)))
    return dict(field=field, fracture_mask=fracture_mask, dilation=dilation, conv_weight=conv_weight, embed_weight=embed_weight, qkv_weight=qkv_weight, out_grad=out_grad)


def apply_offsets(padded, weight, dilate, direction, dims_out):
    x_cells, y_cells, z_cells, channels = dims_out
    summed = jnp.zeros((x_cells * y_cells * z_cells, weight.shape[-1]), jnp.float32)
    for offset_x in (-1, 0, 1):
        for offset_y in (-1, 0, 1):
            for offset_z in (-1, 0, 1):
                tap_index = 9 * (offset_x + 1) + 3 * (offset_y + 1) + offset_z + 1
                anchor = (
                    (DMAX + direction * offset_x * dilate[0]).astype(jnp.int32),
                    (DMAX + direction * offset_y * dilate[1]).astype(jnp.int32),
                    (DMAX + direction * offset_z * dilate[2]).astype(jnp.int32),
                    jnp.int32(0),
                )
                window = lax.dynamic_slice(padded, anchor, (x_cells, y_cells, z_cells, channels))
                summed = summed + jnp.dot(
                    window.reshape(-1, channels),
                    weight[tap_index * channels:(tap_index + 1) * channels],
                    preferred_element_type=jnp.float32,
                )
    return summed.reshape(x_cells, y_cells, z_cells, -1)


def head_grads(items):
    query_h, key_h, value_h, grad_h = items
    inv_root = HD ** -0.5
    scores = jnp.dot(query_h, key_h.T, preferred_element_type=jnp.float32) * inv_root
    top_score = jnp.max(scores, axis=1, keepdims=True)
    expo = jnp.exp(scores - top_score)
    probs = expo / jnp.sum(expo, axis=1, keepdims=True)
    probs_b = probs.astype(jnp.bfloat16)
    attended = jnp.dot(probs_b, value_h, preferred_element_type=jnp.float32)
    row_delta = jnp.sum(grad_h.astype(jnp.float32) * attended, axis=1, keepdims=True)
    score_grad = jnp.dot(grad_h, value_h.T, preferred_element_type=jnp.float32)
    dscore = (probs * (score_grad - row_delta) * inv_root).astype(jnp.bfloat16)
    grad_query = jnp.dot(dscore, key_h, preferred_element_type=jnp.float32).astype(jnp.bfloat16)
    grad_key = jnp.dot(dscore.T, query_h, preferred_element_type=jnp.float32).astype(jnp.bfloat16)
    grad_value = jnp.dot(probs_b.T, grad_h, preferred_element_type=jnp.float32).astype(jnp.bfloat16)
    return grad_query, grad_key, grad_value


def by_heads(matrix):
    return matrix.reshape(TOKENS, HEADS, HD).transpose(1, 0, 2)


def from_heads(stacked):
    return stacked.transpose(1, 0, 2).reshape(TOKENS, D)


def reference(field, fracture_mask, dilation, conv_weight, embed_weight, qkv_weight, out_grad):
    margins = ((DMAX, DMAX), (DMAX, DMAX), (DMAX, DMAX), (0, 0))
    gate_mask = fracture_mask.astype(jnp.float32)[..., None]
    hidden = field
    conv_outs = []
    for layer_num in range(LAYERS):
        conv_out = apply_offsets(jnp.pad(hidden, margins), conv_weight[layer_num], dilation[layer_num], 1, hidden.shape)
        conv_outs.append(conv_out)
        hidden = (hidden.astype(jnp.float32) + gate_mask * (conv_out * jax.nn.sigmoid(conv_out))).astype(jnp.bfloat16)
    patches = hidden.reshape(NX // PX, PX, NY // PY, PY, NZ // PZ, PZ, C).transpose(0, 2, 4, 1, 3, 5, 6).reshape(TOKENS, FEAT)
    embed_flat = embed_weight.reshape(FEAT, D)
    tokens = jnp.dot(patches, embed_flat, preferred_element_type=jnp.float32).astype(jnp.bfloat16)
    query = jnp.dot(tokens, qkv_weight[0], preferred_element_type=jnp.float32).astype(jnp.bfloat16)
    key = jnp.dot(tokens, qkv_weight[1], preferred_element_type=jnp.float32).astype(jnp.bfloat16)
    value = jnp.dot(tokens, qkv_weight[2], preferred_element_type=jnp.float32).astype(jnp.bfloat16)
    grad_query, grad_key, grad_value = lax.map(head_grads, (by_heads(query), by_heads(key), by_heads(value), by_heads(out_grad)))
    grad_tokens = (
        jnp.dot(from_heads(grad_query), qkv_weight[0].T, preferred_element_type=jnp.float32)
        + jnp.dot(from_heads(grad_key), qkv_weight[1].T, preferred_element_type=jnp.float32)
        + jnp.dot(from_heads(grad_value), qkv_weight[2].T, preferred_element_type=jnp.float32)
    ).astype(jnp.bfloat16)
    patch_grad = jnp.dot(grad_tokens, embed_flat.T, preferred_element_type=jnp.float32).astype(jnp.bfloat16)
    grid_grad = patch_grad.reshape(NX // PX, NY // PY, NZ // PZ, PX, PY, PZ, C).transpose(0, 3, 1, 4, 2, 5, 6).reshape(NX, NY, NZ, C)
    for layer_num in reversed(range(LAYERS)):
        conv_out = conv_outs[layer_num]
        sigma = jax.nn.sigmoid(conv_out)
        slope_grad = (gate_mask * sigma * (1.0 + conv_out * (1.0 - sigma)) * grid_grad.astype(jnp.float32)).astype(jnp.bfloat16)
        flipped = conv_weight[layer_num].reshape(27, C, C).transpose(0, 2, 1).reshape(27 * C, C)
        backward = apply_offsets(jnp.pad(slope_grad, margins), flipped, dilation[layer_num], -1, slope_grad.shape)
        grid_grad = (grid_grad.astype(jnp.float32) + backward).astype(jnp.bfloat16)
    return grid_grad
```

```python
import functools

import jax
import jax.numpy as jnp
from jax import lax
from jax.experimental import pallas as pl
from jax.experimental.pallas import tpu as pltpu
from jax.sharding import PartitionSpec as P

HD = 128
PY = 8
PZ = 2
LAYERS = 2
DMAX = 2


def padded_2(cells, sides, width):
    for axis, dim in sides:
        count = lax.axis_size(axis)
        ends = count - 1
        head = lax.slice_in_dim(cells, 0, width, axis=dim)
        tail = lax.slice_in_dim(cells, cells.shape[dim] - width, cells.shape[dim], axis=dim)
        cells = jnp.concatenate(
            [
                lax.ppermute(tail, axis, [(i, (i + 1) % count) for i in range(ends)]),
                cells,
                lax.ppermute(head, axis, [((i + 1) % count, i) for i in range(ends)]),
            ],
            axis=dim,
        )
    return cells


def with_rim(volume):
    padded = padded_2(volume, (("zslab", 2), ("blk", 0)), DMAX)
    return jnp.pad(padded, ((0, 0), (DMAX, DMAX), (0, 0), (0, 0)))


def apply_offsets(padded, weight, dilate, direction, dims_out):
    x_cells, y_cells, z_cells, channels = dims_out
    summed = jnp.zeros((x_cells * y_cells * z_cells, weight.shape[-1]), jnp.float32)
    for offset_x in (-1, 0, 1):
        pieces = []
        for offset_y in (-1, 0, 1):
            for offset_z in (-1, 0, 1):
                anchor = (
                    DMAX + direction * offset_x * dilate[0],
                    DMAX + direction * offset_y * dilate[1],
                    DMAX + direction * offset_z * dilate[2],
                    jnp.int32(0),
                )
                pieces.append(
                    lax.dynamic_slice(padded, anchor, (x_cells, y_cells, z_cells, channels))
                )
        stacked = jnp.concatenate(pieces, axis=3).reshape(x_cells * y_cells * z_cells, 9 * channels)
        group_rows = weight[(offset_x + 1) * 9 * channels : (offset_x + 2) * 9 * channels]
        summed = summed + jnp.dot(stacked, group_rows, preferred_element_type=jnp.float32)
    return summed.reshape(x_cells, y_cells, z_cells, -1)


def slab_total(term):
    return lax.psum(term.astype(jnp.bfloat16), "zslab").astype(jnp.float32)


def local(field, fracture_mask, dilation, conv_weight, embed_weight, qkv_weight, out_grad):
    x_cells, y_cells, z_cells, channels = field.shape
    gate_mask = fracture_mask.astype(jnp.float32)[..., None]
    hidden = field
    conv_outs = []
    for layer_num in range(LAYERS):
        conv_out = apply_offsets(
            with_rim(hidden), conv_weight[layer_num], dilation[layer_num], 1, field.shape
        )
        conv_outs.append(conv_out)
        hidden = (
            hidden.astype(jnp.float32) + gate_mask * (conv_out * jax.nn.sigmoid(conv_out))
        ).astype(jnp.bfloat16)
    slab_view = lax.all_to_all(hidden, "zslab", split_axis=0, concat_axis=2, tiled=True)
    x_local, z_total = (slab_view.shape[0], slab_view.shape[2])
    y_blocks, z_blocks = (y_cells // PY, z_total // PZ)
    patches = slab_view.reshape(x_local, y_blocks, PY, z_blocks, PZ, channels).transpose(
        1, 3, 0, 2, 4, 5
    )
    patches = patches.reshape(y_blocks * z_blocks, x_local, PY * PZ * channels)
    embed_rows, qkv_rows = (
        lax.all_gather(embed_weight, "blk", axis=1, tiled=True),
        lax.all_gather(qkv_weight, "blk", axis=1, tiled=True),
    )
    partial_value = jnp.einsum(
        "tpf,pfd->td", patches, embed_rows, preferred_element_type=jnp.float32
    )
    tokens = slab_total(partial_value).astype(jnp.bfloat16)
    projected = jnp.einsum(
        "td,sde->ste", tokens, qkv_rows, preferred_element_type=jnp.float32
    ).astype(jnp.bfloat16)
    key_rows, value_rows = (
        lax.all_gather(projected[1], "blk", axis=0, tiled=True),
        lax.all_gather(projected[2], "blk", axis=0, tiled=True),
    )
    tok_rows = tokens.shape[0]
    head_cols = projected.shape[2]
    heads_here = head_cols // HD
    inv_root = HD ** (-0.5)
    queries = projected[0].reshape(tok_rows, heads_here, HD)
    key_all = key_rows.reshape(-1, heads_here, HD)
    value_all = value_rows.reshape(-1, heads_here, HD)
    grad_out = out_grad.reshape(tok_rows, heads_here, HD)
    scores = (
        jnp.einsum("qhd,khd->hqk", queries, key_all, preferred_element_type=jnp.float32) * inv_root
    )
    top_score = jnp.max(scores, axis=2, keepdims=True)
    expo = jnp.exp(scores - top_score)
    total = jnp.sum(expo, axis=2, keepdims=True)
    probs = expo / total
    probs_b = probs.astype(jnp.bfloat16)
    attended = jnp.einsum("hqk,khd->qhd", probs_b, value_all, preferred_element_type=jnp.float32)
    row_delta = jnp.sum(grad_out.astype(jnp.float32) * attended, axis=2).T[:, :, None]
    score_grad = jnp.einsum("qhd,khd->hqk", grad_out, value_all, preferred_element_type=jnp.float32)
    dscore = (probs * (score_grad - row_delta) * inv_root).astype(jnp.bfloat16)
    grad_query = jnp.einsum("hqk,khd->qhd", dscore, key_all, preferred_element_type=jnp.float32)
    grad_query = grad_query.astype(jnp.bfloat16).reshape(tok_rows, head_cols)
    key_term = jnp.einsum("hqk,qhd->khd", dscore, queries, preferred_element_type=jnp.float32)
    value_term = jnp.einsum("hqk,qhd->khd", probs_b, grad_out, preferred_element_type=jnp.float32)
    key_value_grad = lax.psum_scatter(
        jnp.concatenate(
            [
                key_term.reshape(lax.axis_size("blk") * tok_rows, head_cols),
                value_term.reshape(lax.axis_size("blk") * tok_rows, head_cols),
            ],
            axis=1,
        ).astype(jnp.bfloat16),
        "blk",
        scatter_dimension=0,
        tiled=True,
    )
    grad_key = key_value_grad[:, :head_cols]
    grad_value = key_value_grad[:, head_cols:]
    stacked_grads = jnp.stack([grad_query, grad_key, grad_value])
    embed_rows, qkv_rows = (
        lax.all_gather(embed_weight, "blk", axis=1, tiled=True),
        lax.all_gather(qkv_weight, "blk", axis=1, tiled=True),
    )
    partial_grad = jnp.einsum(
        "ste,sde->td", stacked_grads, qkv_rows, preferred_element_type=jnp.float32
    )
    grad_tokens = slab_total(partial_grad).astype(jnp.bfloat16)
    patch_grad = jnp.einsum(
        "td,pfd->tpf", grad_tokens, embed_rows, preferred_element_type=jnp.float32
    ).astype(jnp.bfloat16)
    grid_grad = patch_grad.reshape(y_blocks, z_blocks, x_local, PY, PZ, channels).transpose(
        2, 0, 3, 1, 4, 5
    )
    grid_grad = grid_grad.reshape(x_local, y_cells, z_total, channels)
    grid_grad = lax.all_to_all(grid_grad, "zslab", split_axis=2, concat_axis=0, tiled=True)
    for layer_num in reversed(range(LAYERS)):
        conv_out = conv_outs[layer_num]
        sigma = jax.nn.sigmoid(conv_out)
        slope_grad = (
            gate_mask * sigma * (1.0 + conv_out * (1.0 - sigma)) * grid_grad.astype(jnp.float32)
        ).astype(jnp.bfloat16)
        flipped = (
            conv_weight[layer_num]
            .reshape(27, channels, channels)
            .transpose(0, 2, 1)
            .reshape(27 * channels, channels)
        )
        backward = apply_offsets(
            with_rim(slope_grad), flipped, dilation[layer_num], -1, field.shape
        )
        grid_grad = (grid_grad.astype(jnp.float32) + backward).astype(jnp.bfloat16)
    return grid_grad


HALO = [(dz, dx) for dz in (-1, 0, 1) for dx in (-1, 0, 1) if (dz, dx) != (0, 0)]
ZS = 4
NB = 8
ND = ZS * NB
ZC, XC, YC, C = 4, 8, 16, 128
CELLS = ZC * XC * YC
F32 = jnp.float32
BF16 = jnp.bfloat16
CONTRACT_LAST = (((1,), (1,)), ((), ()))


def one_hot(target):
    rows = lax.broadcasted_iota(jnp.int32, (CELLS, 1), 0)
    cols = lax.broadcasted_iota(jnp.int32, (CELLS, CELLS), 1)
    return jnp.where(cols == target(rows), 1.0, 0.0).astype(F32).astype(BF16)


def bit(value, low, count):
    return (value >> low) & ((1 << count) - 1)


def cell_of_slot(r):
    zs, py, px_lo, pz, yp, zp_lo = (
        bit(r, 7, 2), bit(r, 4, 3), bit(r, 3, 1), bit(r, 2, 1), bit(r, 1, 1), bit(r, 0, 1)
    )
    return (zp_lo * 2 + pz) * 128 + (2 * zs + px_lo) * 16 + yp * 8 + py


def slot_of_cell(r):
    zp_lo, pz, zs, px_lo, yp, py = (
        bit(r, 8, 1), bit(r, 7, 1), bit(r, 5, 2), bit(r, 4, 1), bit(r, 3, 1), bit(r, 0, 3)
    )
    return (zs * 8 + py) * 16 + px_lo * 8 + pz * 4 + yp * 2 + zp_lo


def arrival_of_row(r):
    q, xp, yp, zs, zp_lo = bit(r, 7, 2), bit(r, 4, 3), bit(r, 3, 1), bit(r, 1, 2), bit(r, 0, 1)
    return (zs * 8 + xp) * 16 + q * 4 + yp * 2 + zp_lo


def row_of_arrival(r):
    zs, xp, q, yp, zp_lo = bit(r, 7, 2), bit(r, 4, 3), bit(r, 2, 2), bit(r, 1, 1), bit(r, 0, 1)
    return q * 128 + xp * 16 + yp * 8 + zs * 2 + zp_lo


def sigmoid(a):
    return 1.0 / (1.0 + jnp.exp(-a))


def span(step, size):
    if step == 0:
        return 2, 2, size
    return (size, 0, 2) if step == 1 else (2, size + 2, 2)


def kernel(
    dilation, field, mask, conv_hbm, embed_hbm, qkv_hbm, grad_hbm, out,
    pads, taps, conv_w, embed, weights, grads, conv_outs,
    send_patch, got_patch, send_part, got_part, tokens,
    send_gt, got_gt, grad_tok, send_back, got_back,
    halo_send, halo_recv, load_sem, qkv_send, qkv_recv, fwd_send, fwd_recv,
    og_send, og_recv, all_send, all_recv, gt_send, gt_recv,
):
    zs, b = lax.axis_index("zslab"), lax.axis_index("blk")
    me = zs * NB + b
    partner = b + 1 - 2 * lax.rem(b, 2)

    loads = [
        pltpu.make_async_copy(conv_hbm, conv_w, load_sem.at[0]),
        pltpu.make_async_copy(embed_hbm, embed, load_sem.at[1]),
        pltpu.make_async_copy(qkv_hbm, weights.at[b], load_sem.at[2]),
        pltpu.make_async_copy(grad_hbm, grads.at[b], load_sem.at[3]),
    ]
    for load in loads:
        load.start()

    pads[...] = jnp.zeros_like(pads)
    barrier = pltpu.get_barrier_semaphore()

    @pl.loop(1, ND)
    def _(d):
        peer = lax.rem(me + d, ND)
        pl.semaphore_signal(
            barrier, inc=1, device_id=(peer // NB, lax.rem(peer, NB)),
            device_id_type=pl.DeviceIdType.MESH,
        )

    pl.semaphore_wait(barrier, ND - 1)

    def remote(src, dst, send, recv, to):
        return pltpu.make_async_remote_copy(
            src_ref=src, dst_ref=dst, send_sem=send, recv_sem=recv,
            device_id=to, device_id_type=pl.DeviceIdType.MESH,
        )

    def halo_copy(n, d):
        dz, dx = HALO[d]
        z0, z1, zl = span(dz, ZC)
        x0, x1, xl = span(dx, XC)
        return remote(
            pads.at[n, pl.ds(z0, zl), pl.ds(x0, xl)], pads.at[n, pl.ds(z1, zl), pl.ds(x1, xl)],
            halo_send.at[n, d], halo_recv.at[n, d],
            (lax.rem(zs + dz + ZS, ZS), lax.rem(b + dx + NB, NB)),
        )

    def inside(dz, dx):
        return (zs + dz >= 0) & (zs + dz < ZS) & (b + dx >= 0) & (b + dx < NB)

    def send_halo(n, cells):
        pads[n, 2:6, 2:10] = cells.reshape(ZC, XC, YC, C)
        for d, (dz, dx) in enumerate(HALO):
            @pl.when(inside(dz, dx))
            def _():
                halo_copy(n, d).start()

    def wait_halo(n):
        for d, (dz, dx) in enumerate(HALO):
            @pl.when(inside(-dz, -dx))
            def _():
                halo_copy(n, d).wait_recv()

            @pl.when(inside(dz, dx))
            def _():
                halo_copy(n, d).wait_send()

    def convolve(n, layer, direction):
        rx, ry, rz = dilation[layer, 0], dilation[layer, 1], dilation[layer, 2]
        rows = (ZC + 4) * (XC + 4) * YC
        flat = pads[n].reshape(rows, C).astype(F32)
        y = lax.broadcasted_iota(jnp.int32, (rows, C), 0) & (YC - 1)

        def shifted(by):
            near = pltpu.roll(flat, (-by) % rows, 0)
            far = pltpu.roll(flat, (-2 * by) % rows, 0)
            moved = jnp.where(ry == 1, near, far)
            source = y + by * ry
            return jnp.where((source >= 0) & (source < YC), moved, 0.0)

        for j, value in ((0, shifted(-direction)), (1, flat), (2, shifted(direction))):
            taps[:, :, :, j * C:(j + 1) * C] = value.astype(BF16).reshape(
                ZC + 4, XC + 4, YC, C
            )
        total = jnp.zeros((CELLS, C), F32)
        for i in (-1, 0, 1):
            for k in (-1, 0, 1):
                lhs = taps[
                    pl.ds(2 + direction * k * rz, ZC), pl.ds(2 + direction * i * rx, XC)
                ].reshape(CELLS, 3 * C)
                rows_at = [(9 * (i + 1) + 3 * j + k + 1) * C for j in range(3)]
                parts = [conv_w[layer, at:at + C, :] for at in rows_at]
                if direction == 1:
                    total += jnp.dot(
                        lhs, jnp.concatenate(parts, axis=0), preferred_element_type=F32
                    )
                else:
                    total += lax.dot_general(
                        lhs, jnp.concatenate(parts, axis=1), CONTRACT_LAST,
                        preferred_element_type=F32,
                    )
        return total

    def all_copy(phase, d, src, dst):
        peer = lax.rem(me + d, ND)
        return remote(
            src, dst, all_send.at[phase, d], all_recv.at[phase, d],
            (peer // NB, lax.rem(peer, NB)),
        )

    def scatter(phase, sends, gets):
        @pl.loop(1, ND)
        def _(d):
            all_copy(phase, d, sends.at[lax.rem(me + d, ND)], gets.at[me]).start()

        gets[pl.ds(me, 1)] = sends[pl.ds(me, 1)]

    def scatter_wait(phase, sends, gets):
        @pl.loop(1, ND)
        def _(d):
            copy = all_copy(
                phase, d, sends.at[lax.rem(me + d, ND)], gets.at[lax.rem(me - d + ND, ND)]
            )
            copy.wait_recv()
            copy.wait_send()

    send_halo(0, field[...])

    def qkv_copy(d):
        return remote(
            qkv_hbm, weights.at[b], qkv_send.at[d], qkv_recv.at[d],
            (zs, partner if d == 0 else lax.rem(b + 2 * d, NB)),
        )

    def qkv_forward(d):
        held = weights.at[lax.rem(b - 2 * d + NB, NB)]
        return remote(held, held, fwd_send.at[d], fwd_recv.at[d], (zs, partner))

    def grad_copy(d):
        return remote(
            grad_hbm, grads.at[b], og_send.at[d], og_recv.at[d], (zs, lax.rem(b + d, NB))
        )

    for d in range(NB // 2):
        qkv_copy(d).start()
    for d in range(1, NB):
        grad_copy(d).start()

    gate = mask[...]
    loads[0].wait()
    hidden = field[...].reshape(CELLS, C)
    for layer in range(LAYERS):
        if layer:
            send_halo(layer, hidden)
        wait_halo(layer)
        conv_out = convolve(layer, layer, 1)
        conv_outs[layer] = conv_out
        hidden = (hidden.astype(F32) + gate * (conv_out * sigmoid(conv_out))).astype(BF16)

    send_patch[...] = (
        jnp.dot(one_hot(cell_of_slot), hidden, preferred_element_type=F32)
        .astype(BF16).reshape(ND, 16, C)
    )
    scatter(0, send_patch, got_patch)
    for d in range(1, NB // 2):
        qkv_copy(d).wait_recv()
        qkv_forward(d).start()
    loads[1].wait()
    gather_rows = one_hot(arrival_of_row)
    scatter_wait(0, send_patch, got_patch)
    ordered = jnp.dot(
        gather_rows, got_patch[...].reshape(CELLS, C), preferred_element_type=F32
    ).astype(BF16)
    patches = jnp.concatenate([ordered[q * 128:(q + 1) * 128] for q in range(4)], axis=1)
    for part in range(ZS):
        columns = slice(part * 256, (part + 1) * 256)
        send_part[part * NB:(part + 1) * NB] = (
            jnp.dot(patches, embed[:, columns], preferred_element_type=F32)
            .astype(BF16).reshape(NB, 16, 256)
        )
    scatter(1, send_part, got_part)
    scatter_wait(1, send_part, got_part)
    tokens[pl.ds(me, 1)] = (
        jnp.sum(got_part[...].astype(F32), axis=0, keepdims=True).astype(BF16)
    )

    @pl.loop(1, ND)
    def _(d):
        all_copy(2, d, tokens.at[me], tokens.at[me]).start()

    for load in loads[2:]:
        load.wait()
    qkv_copy(0).wait()
    for d in range(1, NB // 2):
        qkv_copy(d).wait_send()
        qkv_forward(d).wait_send()
        remote(
            qkv_hbm, weights.at[lax.rem(partner - 2 * d + NB, NB)],
            fwd_send.at[d], fwd_recv.at[d], (zs, partner),
        ).wait_recv()
    for d in range(1, NB):
        grad_copy(d).wait()

    @pl.loop(1, ND)
    def _(d):
        held = tokens.at[lax.rem(me - d + ND, ND)]
        copy = all_copy(2, d, held, held)
        copy.wait_recv()
        copy.wait_send()

    all_tokens = jnp.concatenate(
        [tokens[part * NB:(part + 1) * NB].reshape(128, 256) for part in range(ZS)], axis=1
    )
    projected = [
        jnp.dot(all_tokens, weights[:, s].reshape(1024, 256), preferred_element_type=F32)
        .astype(BF16)
        for s in range(3)
    ]
    grad_out = grads[...].reshape(128, 256)
    inv_root = HD ** (-0.5)
    pieces = []
    for head in range(2):
        columns = slice(head * HD, (head + 1) * HD)
        query, key, value = (array[:, columns] for array in projected)
        grad_h = grad_out[:, columns]
        scores = lax.dot_general(query, key, CONTRACT_LAST, preferred_element_type=F32) * inv_root
        expo = jnp.exp(scores - jnp.max(scores, axis=1, keepdims=True))
        probs = expo / jnp.sum(expo, axis=1, keepdims=True)
        probs_b = probs.astype(BF16)
        attended = jnp.dot(probs_b, value, preferred_element_type=F32)
        row_delta = jnp.sum(grad_h.astype(F32) * attended, axis=1, keepdims=True)
        score_grad = lax.dot_general(grad_h, value, CONTRACT_LAST, preferred_element_type=F32)
        dscore = probs * (score_grad - row_delta) * inv_root
        dscore_t = dscore.T.astype(BF16)
        probs_t = probs.T.astype(BF16)
        pieces.append((
            jnp.dot(dscore.astype(BF16), key, preferred_element_type=F32).astype(BF16),
            jnp.dot(dscore_t, query, preferred_element_type=F32).astype(BF16),
            jnp.dot(probs_t, grad_h, preferred_element_type=F32).astype(BF16),
        ))
    stacked = [jnp.concatenate([piece[s] for piece in pieces], axis=1) for s in range(3)]
    for part in range(ZS):
        term = jnp.zeros((128, 256), F32)
        for s in range(3):
            rows = weights[part * 2:part * 2 + 2, s].reshape(256, 256)
            term += lax.dot_general(stacked[s], rows, CONTRACT_LAST, preferred_element_type=F32)
        send_gt[part] = term.astype(BF16)

    def slab_copy(phase, d, src, dst):
        return remote(
            src, dst, gt_send.at[phase, d], gt_recv.at[phase, d], (lax.rem(zs + d, ZS), b)
        )

    for d in range(1, ZS):
        slab_copy(0, d, send_gt.at[lax.rem(zs + d, ZS)], got_gt.at[zs]).start()
    got_gt[pl.ds(zs, 1)] = send_gt[pl.ds(zs, 1)]
    for d in range(1, ZS):
        slab_copy(
            0, d, send_gt.at[lax.rem(zs + d, ZS)], got_gt.at[lax.rem(zs - d + ZS, ZS)]
        ).wait()
    grad_tok[pl.ds(zs, 1)] = (
        jnp.sum(got_gt[...].astype(F32), axis=0, keepdims=True).astype(BF16)
    )
    for d in range(1, ZS):
        slab_copy(1, d, grad_tok.at[zs], grad_tok.at[zs]).start()
    scatter_rows = one_hot(row_of_arrival)
    for d in range(1, ZS):
        held = grad_tok.at[lax.rem(zs - d + ZS, ZS)]
        slab_copy(1, d, held, held).wait()
    all_grad = jnp.concatenate([grad_tok[part] for part in range(ZS)], axis=1)
    patch_grad = jnp.concatenate(
        [
            lax.dot_general(
                all_grad, embed[q * 128:(q + 1) * 128, :], CONTRACT_LAST,
                preferred_element_type=F32,
            ).astype(BF16)
            for q in range(4)
        ],
        axis=0,
    )
    send_back[...] = (
        jnp.dot(scatter_rows, patch_grad, preferred_element_type=F32)
        .astype(BF16).reshape(ND, 16, C)
    )
    scatter(3, send_back, got_back)
    to_cells = one_hot(slot_of_cell)
    scatter_wait(3, send_back, got_back)
    grid_grad = jnp.dot(to_cells, got_back[...].reshape(CELLS, C), preferred_element_type=F32)
    for layer in reversed(range(LAYERS)):
        conv_out = conv_outs[layer]
        sigma = sigmoid(conv_out)
        slope = gate * sigma * (1.0 + conv_out * (1.0 - sigma)) * grid_grad
        n = 2 * LAYERS - 1 - layer
        send_halo(n, slope.astype(BF16))
        wait_halo(n)
        grid_grad = (grid_grad + convolve(n, layer, -1)).astype(BF16).astype(F32)
    out[...] = grid_grad.astype(BF16).reshape(ZC, XC, YC, C)


def fused(field, fracture_mask, dilation, conv_weight, embed_weight, qkv_weight, out_grad):
    cells = field.transpose(2, 0, 1, 3)
    gate = jnp.broadcast_to(
        fracture_mask.transpose(2, 0, 1).reshape(CELLS, 1).astype(F32), (CELLS, C)
    )
    vmem = pl.BlockSpec(memory_space=pltpu.VMEM)
    hbm = pl.BlockSpec(memory_space=pl.ANY)
    dma = pltpu.SemaphoreType.DMA
    result = pl.pallas_call(
        kernel,
        out_shape=jax.ShapeDtypeStruct(cells.shape, BF16),
        in_specs=[pl.BlockSpec(memory_space=pltpu.SMEM), vmem, vmem, hbm, hbm, hbm, hbm],
        out_specs=vmem,
        scratch_shapes=[
            pltpu.VMEM((2 * LAYERS, ZC + 4, XC + 4, YC, C), BF16),
            pltpu.VMEM((ZC + 4, XC + 4, YC, 3 * C), BF16),
            pltpu.VMEM(conv_weight.shape, BF16),
            pltpu.VMEM((512, 1024), BF16),
            pltpu.VMEM((NB, 3, 128, 256), BF16),
            pltpu.VMEM((NB, 16, 256), BF16),
            pltpu.VMEM((LAYERS, CELLS, C), F32),
            pltpu.VMEM((ND, 16, C), BF16),
            pltpu.VMEM((ND, 16, C), BF16),
            pltpu.VMEM((ND, 16, 256), BF16),
            pltpu.VMEM((ND, 16, 256), BF16),
            pltpu.VMEM((ND, 16, 256), BF16),
            pltpu.VMEM((ZS, 128, 256), BF16),
            pltpu.VMEM((ZS, 128, 256), BF16),
            pltpu.VMEM((ZS, 128, 256), BF16),
            pltpu.VMEM((ND, 16, C), BF16),
            pltpu.VMEM((ND, 16, C), BF16),
            dma((2 * LAYERS, 8)),
            dma((2 * LAYERS, 8)),
            dma((4,)),
            dma((NB // 2,)),
            dma((NB // 2,)),
            dma((NB // 2,)),
            dma((NB // 2,)),
            dma((NB,)),
            dma((NB,)),
            dma((4, ND)),
            dma((4, ND)),
            dma((2, ZS)),
            dma((2, ZS)),
        ],
        compiler_params=pltpu.CompilerParams(
            collective_id=0, has_side_effects=True, vmem_limit_bytes=48 * 1024 * 1024
        ),
    )(
        dilation, cells, gate, conv_weight, embed_weight.reshape(512, 1024), qkv_weight, out_grad
    )
    return result.transpose(1, 2, 0, 3)


def block(*arrays):
    field, embed_weight, qkv_weight, out_grad = (arrays[0], arrays[4], arrays[5], arrays[6])
    fits = (
        (lax.axis_size("zslab"), lax.axis_size("blk")) == (ZS, NB)
        and field.shape == (XC, YC, ZC, C)
        and embed_weight.shape == (2, 256, 1024)
        and qkv_weight.shape == (3, 128, 256)
        and out_grad.shape == (16, 256)
    )
    return fused(*arrays) if fits else local(*arrays)


def solution(mesh):
    return jax.shard_map(
        block,
        mesh=mesh,
        in_specs=(
            P("blk", None, "zslab", None),
            P("blk", None, "zslab"),
            P(),
            P(),
            P("zslab", "blk", None),
            P(None, "blk", "zslab"),
            P("blk", "zslab"),
        ),
        out_specs=P("blk", None, "zslab", None),
        check_vma=False,
    )
```

```python
import functools

import jax
import jax.numpy as jnp
from jax import lax
from jax.experimental import pallas as pl
from jax.experimental.pallas import tpu as pltpu
from jax.sharding import PartitionSpec as P

HD = 128
PY = 8
PZ = 2
LAYERS = 2
DMAX = 2


def padded_2(cells, sides, width):
    for axis, dim in sides:
        count = lax.axis_size(axis)
        ends = count - 1
        head = lax.slice_in_dim(cells, 0, width, axis=dim)
        tail = lax.slice_in_dim(cells, cells.shape[dim] - width, cells.shape[dim], axis=dim)
        cells = jnp.concatenate(
            [
                lax.ppermute(tail, axis, [(i, (i + 1) % count) for i in range(ends)]),
                cells,
                lax.ppermute(head, axis, [((i + 1) % count, i) for i in range(ends)]),
            ],
            axis=dim,
        )
    return cells


def with_rim(volume):
    padded = padded_2(volume, (("zslab", 2), ("blk", 0)), DMAX)
    return jnp.pad(padded, ((0, 0), (DMAX, DMAX), (0, 0), (0, 0)))


def apply_offsets(padded, weight, dilate, direction, dims_out):
    x_cells, y_cells, z_cells, channels = dims_out
    summed = jnp.zeros((x_cells * y_cells * z_cells, weight.shape[-1]), jnp.float32)
    for offset_x in (-1, 0, 1):
        pieces = []
        for offset_y in (-1, 0, 1):
            for offset_z in (-1, 0, 1):
                anchor = (
                    DMAX + direction * offset_x * dilate[0],
                    DMAX + direction * offset_y * dilate[1],
                    DMAX + direction * offset_z * dilate[2],
                    jnp.int32(0),
                )
                pieces.append(
                    lax.dynamic_slice(padded, anchor, (x_cells, y_cells, z_cells, channels))
                )
        stacked = jnp.concatenate(pieces, axis=3).reshape(x_cells * y_cells * z_cells, 9 * channels)
        group_rows = weight[(offset_x + 1) * 9 * channels : (offset_x + 2) * 9 * channels]
        summed = summed + jnp.dot(stacked, group_rows, preferred_element_type=jnp.float32)
    return summed.reshape(x_cells, y_cells, z_cells, -1)


def slab_total(term):
    return lax.psum(term.astype(jnp.bfloat16), "zslab").astype(jnp.float32)


def local(field, fracture_mask, dilation, conv_weight, embed_weight, qkv_weight, out_grad):
    x_cells, y_cells, z_cells, channels = field.shape
    gate_mask = fracture_mask.astype(jnp.float32)[..., None]
    hidden = field
    conv_outs = []
    for layer_num in range(LAYERS):
        conv_out = apply_offsets(
            with_rim(hidden), conv_weight[layer_num], dilation[layer_num], 1, field.shape
        )
        conv_outs.append(conv_out)
        hidden = (
            hidden.astype(jnp.float32) + gate_mask * (conv_out * jax.nn.sigmoid(conv_out))
        ).astype(jnp.bfloat16)
    slab_view = lax.all_to_all(hidden, "zslab", split_axis=0, concat_axis=2, tiled=True)
    x_local, z_total = (slab_view.shape[0], slab_view.shape[2])
    y_blocks, z_blocks = (y_cells // PY, z_total // PZ)
    patches = slab_view.reshape(x_local, y_blocks, PY, z_blocks, PZ, channels).transpose(
        1, 3, 0, 2, 4, 5
    )
    patches = patches.reshape(y_blocks * z_blocks, x_local, PY * PZ * channels)
    embed_rows, qkv_rows = (
        lax.all_gather(embed_weight, "blk", axis=1, tiled=True),
        lax.all_gather(qkv_weight, "blk", axis=1, tiled=True),
    )
    partial_value = jnp.einsum(
        "tpf,pfd->td", patches, embed_rows, preferred_element_type=jnp.float32
    )
    tokens = slab_total(partial_value).astype(jnp.bfloat16)
    projected = jnp.einsum(
        "td,sde->ste", tokens, qkv_rows, preferred_element_type=jnp.float32
    ).astype(jnp.bfloat16)
    key_rows, value_rows = (
        lax.all_gather(projected[1], "blk", axis=0, tiled=True),
        lax.all_gather(projected[2], "blk", axis=0, tiled=True),
    )
    tok_rows = tokens.shape[0]
    head_cols = projected.shape[2]
    heads_here = head_cols // HD
    inv_root = HD ** (-0.5)
    queries = projected[0].reshape(tok_rows, heads_here, HD)
    key_all = key_rows.reshape(-1, heads_here, HD)
    value_all = value_rows.reshape(-1, heads_here, HD)
    grad_out = out_grad.reshape(tok_rows, heads_here, HD)
    scores = (
        jnp.einsum("qhd,khd->hqk", queries, key_all, preferred_element_type=jnp.float32) * inv_root
    )
    top_score = jnp.max(scores, axis=2, keepdims=True)
    expo = jnp.exp(scores - top_score)
    total = jnp.sum(expo, axis=2, keepdims=True)
    probs = expo / total
    probs_b = probs.astype(jnp.bfloat16)
    attended = jnp.einsum("hqk,khd->qhd", probs_b, value_all, preferred_element_type=jnp.float32)
    row_delta = jnp.sum(grad_out.astype(jnp.float32) * attended, axis=2).T[:, :, None]
    score_grad = jnp.einsum("qhd,khd->hqk", grad_out, value_all, preferred_element_type=jnp.float32)
    dscore = (probs * (score_grad - row_delta) * inv_root).astype(jnp.bfloat16)
    grad_query = jnp.einsum("hqk,khd->qhd", dscore, key_all, preferred_element_type=jnp.float32)
    grad_query = grad_query.astype(jnp.bfloat16).reshape(tok_rows, head_cols)
    key_term = jnp.einsum("hqk,qhd->khd", dscore, queries, preferred_element_type=jnp.float32)
    value_term = jnp.einsum("hqk,qhd->khd", probs_b, grad_out, preferred_element_type=jnp.float32)
    key_value_grad = lax.psum_scatter(
        jnp.concatenate(
            [
                key_term.reshape(lax.axis_size("blk") * tok_rows, head_cols),
                value_term.reshape(lax.axis_size("blk") * tok_rows, head_cols),
            ],
            axis=1,
        ).astype(jnp.bfloat16),
        "blk",
        scatter_dimension=0,
        tiled=True,
    )
    grad_key = key_value_grad[:, :head_cols]
    grad_value = key_value_grad[:, head_cols:]
    stacked_grads = jnp.stack([grad_query, grad_key, grad_value])
    embed_rows, qkv_rows = (
        lax.all_gather(embed_weight, "blk", axis=1, tiled=True),
        lax.all_gather(qkv_weight, "blk", axis=1, tiled=True),
    )
    partial_grad = jnp.einsum(
        "ste,sde->td", stacked_grads, qkv_rows, preferred_element_type=jnp.float32
    )
    grad_tokens = slab_total(partial_grad).astype(jnp.bfloat16)
    patch_grad = jnp.einsum(
        "td,pfd->tpf", grad_tokens, embed_rows, preferred_element_type=jnp.float32
    ).astype(jnp.bfloat16)
    grid_grad = patch_grad.reshape(y_blocks, z_blocks, x_local, PY, PZ, channels).transpose(
        2, 0, 3, 1, 4, 5
    )
    grid_grad = grid_grad.reshape(x_local, y_cells, z_total, channels)
    grid_grad = lax.all_to_all(grid_grad, "zslab", split_axis=2, concat_axis=0, tiled=True)
    for layer_num in reversed(range(LAYERS)):
        conv_out = conv_outs[layer_num]
        sigma = jax.nn.sigmoid(conv_out)
        slope_grad = (
            gate_mask * sigma * (1.0 + conv_out * (1.0 - sigma)) * grid_grad.astype(jnp.float32)
        ).astype(jnp.bfloat16)
        flipped = (
            conv_weight[layer_num]
            .reshape(27, channels, channels)
            .transpose(0, 2, 1)
            .reshape(27 * channels, channels)
        )
        backward = apply_offsets(
            with_rim(slope_grad), flipped, dilation[layer_num], -1, field.shape
        )
        grid_grad = (grid_grad.astype(jnp.float32) + backward).astype(jnp.bfloat16)
    return grid_grad


HALO = [(dz, dx) for dz in (-1, 0, 1) for dx in (-1, 0, 1) if (dz, dx) != (0, 0)]
ZS = 4
NB = 8
ND = ZS * NB
ZC, XC, YC, C = 4, 8, 16, 128
CELLS = ZC * XC * YC
F32 = jnp.float32
BF16 = jnp.bfloat16
CONTRACT_LAST = (((1,), (1,)), ((), ()))


def one_hot(target):
    rows = lax.broadcasted_iota(jnp.int32, (CELLS, 1), 0)
    cols = lax.broadcasted_iota(jnp.int32, (CELLS, CELLS), 1)
    return jnp.where(cols == target(rows), 1.0, 0.0).astype(F32).astype(BF16)


def bit(value, low, count):
    return (value >> low) & ((1 << count) - 1)


def cell_of_slot(r):
    zs, py, px_lo, pz, yp, zp_lo = (
        bit(r, 7, 2), bit(r, 4, 3), bit(r, 3, 1), bit(r, 2, 1), bit(r, 1, 1), bit(r, 0, 1)
    )
    return (zp_lo * 2 + pz) * 128 + (2 * zs + px_lo) * 16 + yp * 8 + py


def slot_of_cell(r):
    zp_lo, pz, zs, px_lo, yp, py = (
        bit(r, 8, 1), bit(r, 7, 1), bit(r, 5, 2), bit(r, 4, 1), bit(r, 3, 1), bit(r, 0, 3)
    )
    return (zs * 8 + py) * 16 + px_lo * 8 + pz * 4 + yp * 2 + zp_lo


def arrival_of_row(r):
    q, xp, yp, zs, zp_lo = bit(r, 7, 2), bit(r, 4, 3), bit(r, 3, 1), bit(r, 1, 2), bit(r, 0, 1)
    return (zs * 8 + xp) * 16 + q * 4 + yp * 2 + zp_lo


def row_of_arrival(r):
    zs, xp, q, yp, zp_lo = bit(r, 7, 2), bit(r, 4, 3), bit(r, 2, 2), bit(r, 1, 1), bit(r, 0, 1)
    return q * 128 + xp * 16 + yp * 8 + zs * 2 + zp_lo


def sigmoid(a):
    return 1.0 / (1.0 + jnp.exp(-a))


def span(step, size):
    if step == 0:
        return 2, 2, size
    return (size, 0, 2) if step == 1 else (2, size + 2, 2)


def kernel(
    dilation, field, mask, conv_hbm, embed_hbm, qkv_hbm, grad_hbm, out,
    pad_0, pad_1, pad_2, pad_3, gate_ref, orders, conv_w, embed, weights, grads, conv_outs,
    send_patch, got_patch, send_part, got_part, tokens,
    send_gt, got_gt, grad_tok, send_back, got_back,
    halo_send, halo_recv, load_sem, qkv_send, qkv_recv, fwd_send, fwd_recv,
    og_send, og_recv, all_send, all_recv, gt_send, gt_recv,
):
    pads = (pad_0, pad_1, pad_2, pad_3)
    zs, b = lax.axis_index("zslab"), lax.axis_index("blk")
    me = zs * NB + b
    partner = b + 1 - 2 * lax.rem(b, 2)

    loads = [
        pltpu.make_async_copy(conv_hbm, conv_w, load_sem.at[0]),
        pltpu.make_async_copy(embed_hbm, embed, load_sem.at[1]),
        pltpu.make_async_copy(qkv_hbm, weights.at[b], load_sem.at[2]),
        pltpu.make_async_copy(grad_hbm, grads.at[b], load_sem.at[3]),
    ]
    for pad in pads:
        pad[...] = jnp.zeros_like(pad)
    loads += [
        pltpu.make_async_copy(field, pad_0.at[pl.ds(2, ZC), pl.ds(2, XC)], load_sem.at[4]),
        pltpu.make_async_copy(mask, gate_ref, load_sem.at[5]),
    ]
    barrier = pltpu.get_barrier_semaphore()

    @pl.loop(1, ND)
    def _(d):
        peer = lax.rem(me + d, ND)
        pl.semaphore_signal(
            barrier, inc=1, device_id=(peer // NB, lax.rem(peer, NB)),
            device_id_type=pl.DeviceIdType.MESH,
        )

    for load in loads[::-1]:
        load.start()
    for at, target in enumerate((cell_of_slot, arrival_of_row, row_of_arrival, slot_of_cell)):
        orders[at] = one_hot(target)
    loads[4].wait()
    pl.semaphore_wait(barrier, ND - 1)

    def remote(src, dst, send, recv, to):
        return pltpu.make_async_remote_copy(
            src_ref=src, dst_ref=dst, send_sem=send, recv_sem=recv,
            device_id=to, device_id_type=pl.DeviceIdType.MESH,
        )

    def halo_copy(n, d):
        dz, dx = HALO[d]
        z0, z1, zl = span(dz, ZC)
        x0, x1, xl = span(dx, XC)
        return remote(
            pads[n].at[pl.ds(z0, zl), pl.ds(x0, xl)], pads[n].at[pl.ds(z1, zl), pl.ds(x1, xl)],
            halo_send.at[n, d], halo_recv.at[n, d],
            (lax.rem(zs + dz + ZS, ZS), lax.rem(b + dx + NB, NB)),
        )

    def inside(dz, dx):
        return (zs + dz >= 0) & (zs + dz < ZS) & (b + dx >= 0) & (b + dx < NB)

    def send_halo(n):
        for d, (dz, dx) in enumerate(HALO):
            @pl.when(inside(dz, dx))
            def _():
                halo_copy(n, d).start()

    def wait_halo(n):
        for d, (dz, dx) in enumerate(HALO):
            @pl.when(inside(-dz, -dx))
            def _():
                halo_copy(n, d).wait_recv()

    def convolve(n, layer, direction):
        rx, ry, rz = dilation[layer, 0], dilation[layer, 1], dilation[layer, 2]
        places = [(i, k) for i in (-1, 0, 1) for k in (-1, 0, 1)]
        windows = jnp.concatenate(
            [
                pads[n][
                    pl.ds(2 + direction * k * rz, ZC), pl.ds(2 + direction * i * rx, XC)
                ].reshape(CELLS, C)
                for i, k in places
            ],
            axis=1,
        )

        def tap(i, j, k):
            at = (9 * (i + 1) + 3 * j + k + 1) * C
            return conv_w[layer, at:at + C, :]

        if direction == 1:
            matrix = jnp.concatenate(
                [jnp.concatenate([tap(i, j, k) for j in range(3)], axis=1) for i, k in places],
                axis=0,
            )
            summed = jnp.dot(windows, matrix, preferred_element_type=F32)
        else:
            matrix = jnp.concatenate(
                [jnp.concatenate([tap(i, j, k) for i, k in places], axis=1) for j in range(3)],
                axis=0,
            )
            summed = lax.dot_general(
                windows, matrix, CONTRACT_LAST, preferred_element_type=F32
            )
        y = lax.broadcasted_iota(jnp.int32, (CELLS, C), 0) & (YC - 1)

        def shifted(value, by):
            near = pltpu.roll(value, (-by) % CELLS, 0)
            far = pltpu.roll(value, (-2 * by) % CELLS, 0)
            source = y + by * ry
            return jnp.where((source >= 0) & (source < YC), jnp.where(ry == 1, near, far), 0.0)

        return (
            summed[:, C:2 * C]
            + shifted(summed[:, :C], -direction)
            + shifted(summed[:, 2 * C:], direction)
        )

    def all_copy(phase, d, src, dst):
        peer = lax.rem(me + d, ND)
        return remote(
            src, dst, all_send.at[phase], all_recv.at[phase],
            (lax.div(peer, NB), lax.rem(peer, NB)),
        )

    def all_bytes(phase, ref):
        part = ref.at[pl.ds(0, ND - 1)]
        return all_copy(phase, 1, part, part)

    def scatter(phase, sends, gets):
        @pl.loop(1, ND)
        def _(d):
            all_copy(phase, d, sends.at[lax.rem(me + d, ND)], gets.at[me]).start()

        gets[pl.ds(me, 1)] = sends[pl.ds(me, 1)]

    send_halo(0)

    def qkv_copy(d):
        return remote(
            qkv_hbm, weights.at[b], qkv_send.at[d], qkv_recv.at[d],
            (zs, partner if d == 0 else lax.rem(b + 2 * d, NB)),
        )

    def qkv_forward(d):
        held = weights.at[lax.rem(b - 2 * d + NB, NB)]
        return remote(held, held, fwd_send.at[d], fwd_recv.at[d], (zs, partner))

    def grad_copy(d):
        return remote(
            grad_hbm, grads.at[b], og_send.at[d], og_recv.at[d], (zs, lax.rem(b + d, NB))
        )

    for d in range(NB // 2):
        qkv_copy(d).start()
    for d in range(1, NB):
        grad_copy(d).start()

    loads[5].wait()
    gate = gate_ref[...]
    loads[0].wait()
    hidden = pad_0[2:6, 2:10].reshape(CELLS, C)
    for layer in range(LAYERS):
        if layer:
            pads[layer][2:6, 2:10] = hidden.reshape(ZC, XC, YC, C)
            send_halo(layer)
        wait_halo(layer)
        conv_out = convolve(layer, layer, 1)
        conv_outs[layer] = conv_out
        hidden = (hidden.astype(F32) + gate * (conv_out * sigmoid(conv_out))).astype(BF16)

    send_patch[...] = (
        jnp.dot(orders[0], hidden, preferred_element_type=F32)
        .astype(BF16).reshape(ND, 16, C)
    )
    scatter(0, send_patch, got_patch)
    for d in range(1, NB // 2):
        qkv_copy(d).wait_recv()
        qkv_forward(d).start()
    loads[1].wait()
    all_bytes(0, got_patch).wait_recv()
    ordered = jnp.dot(
        orders[1], got_patch[...].reshape(CELLS, C), preferred_element_type=F32
    ).astype(BF16)
    patches = jnp.concatenate([ordered[q * 128:(q + 1) * 128] for q in range(4)], axis=1)
    for part in range(ZS):
        columns = slice(part * 256, (part + 1) * 256)
        send_part[part * NB:(part + 1) * NB] = (
            jnp.dot(patches, embed[:, columns], preferred_element_type=F32)
            .astype(BF16).reshape(NB, 16, 256)
        )
    scatter(1, send_part, got_part)
    all_bytes(1, got_part).wait_recv()
    tokens[pl.ds(me, 1)] = (
        jnp.sum(got_part[...].astype(F32), axis=0, keepdims=True).astype(BF16)
    )

    @pl.loop(1, ND)
    def _(d):
        all_copy(2, d, tokens.at[me], tokens.at[me]).start()

    for load in loads[2:4]:
        load.wait()
    qkv_copy(0).wait_recv()
    for d in range(1, NB // 2):
        remote(
            qkv_hbm, weights.at[lax.rem(partner - 2 * d + NB, NB)],
            fwd_send.at[d], fwd_recv.at[d], (zs, partner),
        ).wait_recv()
    for d in range(1, NB):
        grad_copy(d).wait_recv()
    all_bytes(2, tokens).wait_recv()

    all_tokens = jnp.concatenate(
        [tokens[part * NB:(part + 1) * NB].reshape(128, 256) for part in range(ZS)], axis=1
    )
    projected = [
        jnp.dot(all_tokens, weights[:, s].reshape(1024, 256), preferred_element_type=F32)
        .astype(BF16)
        for s in range(3)
    ]
    grad_out = grads[...].reshape(128, 256)
    inv_root = HD ** (-0.5)
    pieces = []
    for head in range(2):
        columns = slice(head * HD, (head + 1) * HD)
        query, key, value = (array[:, columns] for array in projected)
        grad_h = grad_out[:, columns]
        scores = lax.dot_general(query, key, CONTRACT_LAST, preferred_element_type=F32) * inv_root
        expo = jnp.exp(scores - jnp.max(scores, axis=1, keepdims=True))
        probs = expo / jnp.sum(expo, axis=1, keepdims=True)
        probs_b = probs.astype(BF16)
        attended = jnp.dot(probs_b, value, preferred_element_type=F32)
        row_delta = jnp.sum(grad_h.astype(F32) * attended, axis=1, keepdims=True)
        score_grad = lax.dot_general(grad_h, value, CONTRACT_LAST, preferred_element_type=F32)
        dscore = probs * (score_grad - row_delta) * inv_root
        dscore_t = dscore.T.astype(BF16)
        probs_t = probs.T.astype(BF16)
        pieces.append((
            jnp.dot(dscore.astype(BF16), key, preferred_element_type=F32).astype(BF16),
            jnp.dot(dscore_t, query, preferred_element_type=F32).astype(BF16),
            jnp.dot(probs_t, grad_h, preferred_element_type=F32).astype(BF16),
        ))
    stacked = [jnp.concatenate([piece[s] for piece in pieces], axis=1) for s in range(3)]
    for part in range(ZS):
        term = jnp.zeros((128, 256), F32)
        for s in range(3):
            rows = weights[part * 2:part * 2 + 2, s].reshape(256, 256)
            term += lax.dot_general(stacked[s], rows, CONTRACT_LAST, preferred_element_type=F32)
        send_gt[part] = term.astype(BF16)

    def slab_copy(phase, d, src, dst):
        return remote(
            src, dst, gt_send.at[phase, d], gt_recv.at[phase, d], (lax.rem(zs + d, ZS), b)
        )

    for d in range(1, ZS):
        slab_copy(0, d, send_gt.at[lax.rem(zs + d, ZS)], got_gt.at[zs]).start()
    got_gt[pl.ds(zs, 1)] = send_gt[pl.ds(zs, 1)]
    for d in range(1, ZS):
        slab_copy(
            0, d, send_gt.at[lax.rem(zs + d, ZS)], got_gt.at[lax.rem(zs - d + ZS, ZS)]
        ).wait_recv()
    grad_tok[pl.ds(zs, 1)] = (
        jnp.sum(got_gt[...].astype(F32), axis=0, keepdims=True).astype(BF16)
    )
    for d in range(1, ZS):
        slab_copy(1, d, grad_tok.at[zs], grad_tok.at[zs]).start()
    for d in range(1, ZS):
        held = grad_tok.at[lax.rem(zs - d + ZS, ZS)]
        slab_copy(1, d, held, held).wait_recv()
    all_grad = jnp.concatenate([grad_tok[part] for part in range(ZS)], axis=1)
    patch_grad = jnp.concatenate(
        [
            lax.dot_general(
                all_grad, embed[q * 128:(q + 1) * 128, :], CONTRACT_LAST,
                preferred_element_type=F32,
            ).astype(BF16)
            for q in range(4)
        ],
        axis=0,
    )
    send_back[...] = (
        jnp.dot(orders[2], patch_grad, preferred_element_type=F32)
        .astype(BF16).reshape(ND, 16, C)
    )
    scatter(3, send_back, got_back)
    all_bytes(3, got_back).wait_recv()
    grid_grad = jnp.dot(orders[3], got_back[...].reshape(CELLS, C), preferred_element_type=F32)
    for layer in reversed(range(LAYERS)):
        conv_out = conv_outs[layer]
        sigma = sigmoid(conv_out)
        slope = gate * sigma * (1.0 + conv_out * (1.0 - sigma)) * grid_grad
        n = 2 * LAYERS - 1 - layer
        pads[n][2:6, 2:10] = slope.astype(BF16).reshape(ZC, XC, YC, C)
        send_halo(n)
        wait_halo(n)
        grid_grad = (grid_grad + convolve(n, layer, -1)).astype(BF16).astype(F32)
    out[...] = grid_grad.astype(BF16).reshape(ZC, XC, YC, C)

    for n in range(2 * LAYERS):
        for d, (dz, dx) in enumerate(HALO):
            @pl.when(inside(dz, dx))
            def _():
                halo_copy(n, d).wait_send()
    for d in range(NB // 2):
        qkv_copy(d).wait_send()
        if d:
            qkv_forward(d).wait_send()
    for d in range(1, NB):
        grad_copy(d).wait_send()
    for phase, ref in enumerate((send_patch, send_part, tokens, send_back)):
        all_bytes(phase, ref).wait_send()
    for phase in range(2):
        for d in range(1, ZS):
            slab_copy(phase, d, send_gt.at[0], got_gt.at[0]).wait_send()


def fused(field, fracture_mask, dilation, conv_weight, embed_weight, qkv_weight, out_grad):
    cells = field.transpose(2, 0, 1, 3)
    gate = jnp.broadcast_to(
        fracture_mask.transpose(2, 0, 1).reshape(CELLS, 1).astype(F32), (CELLS, C)
    )
    vmem = pl.BlockSpec(memory_space=pltpu.VMEM)
    hbm = pl.BlockSpec(memory_space=pltpu.HBM)
    dma = pltpu.SemaphoreType.DMA
    result = pl.pallas_call(
        kernel,
        out_shape=jax.ShapeDtypeStruct(cells.shape, BF16),
        in_specs=[pl.BlockSpec(memory_space=pltpu.SMEM)] + [hbm] * 6,
        out_specs=vmem,
        scratch_shapes=[
            *[pltpu.VMEM((ZC + 4, XC + 4, YC, C), BF16)] * (2 * LAYERS),
            pltpu.VMEM((CELLS, C), F32),
            pltpu.VMEM((4, CELLS, CELLS), BF16),
            pltpu.VMEM(conv_weight.shape, BF16),
            pltpu.VMEM((512, 1024), BF16),
            pltpu.VMEM((NB, 3, 128, 256), BF16),
            pltpu.VMEM((NB, 16, 256), BF16),
            pltpu.VMEM((LAYERS, CELLS, C), F32),
            pltpu.VMEM((ND, 16, C), BF16),
            pltpu.VMEM((ND, 16, C), BF16),
            pltpu.VMEM((ND, 16, 256), BF16),
            pltpu.VMEM((ND, 16, 256), BF16),
            pltpu.VMEM((ND, 16, 256), BF16),
            pltpu.VMEM((ZS, 128, 256), BF16),
            pltpu.VMEM((ZS, 128, 256), BF16),
            pltpu.VMEM((ZS, 128, 256), BF16),
            pltpu.VMEM((ND, 16, C), BF16),
            pltpu.VMEM((ND, 16, C), BF16),
            dma((2 * LAYERS, 8)),
            dma((2 * LAYERS, 8)),
            dma((6,)),
            dma((NB // 2,)),
            dma((NB // 2,)),
            dma((NB // 2,)),
            dma((NB // 2,)),
            dma((NB,)),
            dma((NB,)),
            dma((4,)),
            dma((4,)),
            dma((2, ZS)),
            dma((2, ZS)),
        ],
        compiler_params=pltpu.CompilerParams(
            collective_id=0, has_side_effects=True, vmem_limit_bytes=48 * 1024 * 1024
        ),
    )(
        dilation, cells, gate, conv_weight, embed_weight.reshape(512, 1024), qkv_weight, out_grad
    )
    return result.transpose(1, 2, 0, 3)


def block(*arrays):
    field, embed_weight, qkv_weight, out_grad = (arrays[0], arrays[4], arrays[5], arrays[6])
    fits = (
        (lax.axis_size("zslab"), lax.axis_size("blk")) == (ZS, NB)
        and field.shape == (XC, YC, ZC, C)
        and embed_weight.shape == (2, 256, 1024)
        and qkv_weight.shape == (3, 128, 256)
        and out_grad.shape == (16, 256)
    )
    return fused(*arrays) if fits else local(*arrays)


def solution(mesh):
    return jax.shard_map(
        block,
        mesh=mesh,
        in_specs=(
            P("blk", None, "zslab", None),
            P("blk", None, "zslab"),
            P(),
            P(),
            P("zslab", "blk", None),
            P(None, "blk", "zslab"),
            P("blk", "zslab"),
        ),
        out_specs=P("blk", None, "zslab", None),
        check_vma=False,
    )
```

```python
import functools

import jax
import jax.numpy as jnp
from jax import lax
from jax.experimental import pallas as pl
from jax.experimental.pallas import tpu as pltpu
from jax.sharding import PartitionSpec as P

HD = 128
PY = 8
PZ = 2
LAYERS = 2
DMAX = 2


def padded_2(cells, sides, width):
    for axis, dim in sides:
        count = lax.axis_size(axis)
        ends = count - 1
        head = lax.slice_in_dim(cells, 0, width, axis=dim)
        tail = lax.slice_in_dim(cells, cells.shape[dim] - width, cells.shape[dim], axis=dim)
        cells = jnp.concatenate(
            [
                lax.ppermute(tail, axis, [(i, (i + 1) % count) for i in range(ends)]),
                cells,
                lax.ppermute(head, axis, [((i + 1) % count, i) for i in range(ends)]),
            ],
            axis=dim,
        )
    return cells


def with_rim(volume):
    padded = padded_2(volume, (("zslab", 2), ("blk", 0)), DMAX)
    return jnp.pad(padded, ((0, 0), (DMAX, DMAX), (0, 0), (0, 0)))


def apply_offsets(padded, weight, dilate, direction, dims_out):
    x_cells, y_cells, z_cells, channels = dims_out
    summed = jnp.zeros((x_cells * y_cells * z_cells, weight.shape[-1]), jnp.float32)
    for offset_x in (-1, 0, 1):
        pieces = []
        for offset_y in (-1, 0, 1):
            for offset_z in (-1, 0, 1):
                anchor = (
                    DMAX + direction * offset_x * dilate[0],
                    DMAX + direction * offset_y * dilate[1],
                    DMAX + direction * offset_z * dilate[2],
                    jnp.int32(0),
                )
                pieces.append(
                    lax.dynamic_slice(padded, anchor, (x_cells, y_cells, z_cells, channels))
                )
        stacked = jnp.concatenate(pieces, axis=3).reshape(x_cells * y_cells * z_cells, 9 * channels)
        group_rows = weight[(offset_x + 1) * 9 * channels : (offset_x + 2) * 9 * channels]
        summed = summed + jnp.dot(stacked, group_rows, preferred_element_type=jnp.float32)
    return summed.reshape(x_cells, y_cells, z_cells, -1)


def slab_total(term):
    return lax.psum(term.astype(jnp.bfloat16), "zslab").astype(jnp.float32)


def local(field, fracture_mask, dilation, conv_weight, embed_weight, qkv_weight, out_grad):
    x_cells, y_cells, z_cells, channels = field.shape
    gate_mask = fracture_mask.astype(jnp.float32)[..., None]
    hidden = field
    conv_outs = []
    for layer_num in range(LAYERS):
        conv_out = apply_offsets(
            with_rim(hidden), conv_weight[layer_num], dilation[layer_num], 1, field.shape
        )
        conv_outs.append(conv_out)
        hidden = (
            hidden.astype(jnp.float32) + gate_mask * (conv_out * jax.nn.sigmoid(conv_out))
        ).astype(jnp.bfloat16)
    slab_view = lax.all_to_all(hidden, "zslab", split_axis=0, concat_axis=2, tiled=True)
    x_local, z_total = (slab_view.shape[0], slab_view.shape[2])
    y_blocks, z_blocks = (y_cells // PY, z_total // PZ)
    patches = slab_view.reshape(x_local, y_blocks, PY, z_blocks, PZ, channels).transpose(
        1, 3, 0, 2, 4, 5
    )
    patches = patches.reshape(y_blocks * z_blocks, x_local, PY * PZ * channels)
    embed_rows, qkv_rows = (
        lax.all_gather(embed_weight, "blk", axis=1, tiled=True),
        lax.all_gather(qkv_weight, "blk", axis=1, tiled=True),
    )
    partial_value = jnp.einsum(
        "tpf,pfd->td", patches, embed_rows, preferred_element_type=jnp.float32
    )
    tokens = slab_total(partial_value).astype(jnp.bfloat16)
    projected = jnp.einsum(
        "td,sde->ste", tokens, qkv_rows, preferred_element_type=jnp.float32
    ).astype(jnp.bfloat16)
    key_rows, value_rows = (
        lax.all_gather(projected[1], "blk", axis=0, tiled=True),
        lax.all_gather(projected[2], "blk", axis=0, tiled=True),
    )
    tok_rows = tokens.shape[0]
    head_cols = projected.shape[2]
    heads_here = head_cols // HD
    inv_root = HD ** (-0.5)
    queries = projected[0].reshape(tok_rows, heads_here, HD)
    key_all = key_rows.reshape(-1, heads_here, HD)
    value_all = value_rows.reshape(-1, heads_here, HD)
    grad_out = out_grad.reshape(tok_rows, heads_here, HD)
    scores = (
        jnp.einsum("qhd,khd->hqk", queries, key_all, preferred_element_type=jnp.float32) * inv_root
    )
    top_score = jnp.max(scores, axis=2, keepdims=True)
    expo = jnp.exp(scores - top_score)
    total = jnp.sum(expo, axis=2, keepdims=True)
    probs = expo / total
    probs_b = probs.astype(jnp.bfloat16)
    attended = jnp.einsum("hqk,khd->qhd", probs_b, value_all, preferred_element_type=jnp.float32)
    row_delta = jnp.sum(grad_out.astype(jnp.float32) * attended, axis=2).T[:, :, None]
    score_grad = jnp.einsum("qhd,khd->hqk", grad_out, value_all, preferred_element_type=jnp.float32)
    dscore = (probs * (score_grad - row_delta) * inv_root).astype(jnp.bfloat16)
    grad_query = jnp.einsum("hqk,khd->qhd", dscore, key_all, preferred_element_type=jnp.float32)
    grad_query = grad_query.astype(jnp.bfloat16).reshape(tok_rows, head_cols)
    key_term = jnp.einsum("hqk,qhd->khd", dscore, queries, preferred_element_type=jnp.float32)
    value_term = jnp.einsum("hqk,qhd->khd", probs_b, grad_out, preferred_element_type=jnp.float32)
    key_value_grad = lax.psum_scatter(
        jnp.concatenate(
            [
                key_term.reshape(lax.axis_size("blk") * tok_rows, head_cols),
                value_term.reshape(lax.axis_size("blk") * tok_rows, head_cols),
            ],
            axis=1,
        ).astype(jnp.bfloat16),
        "blk",
        scatter_dimension=0,
        tiled=True,
    )
    grad_key = key_value_grad[:, :head_cols]
    grad_value = key_value_grad[:, head_cols:]
    stacked_grads = jnp.stack([grad_query, grad_key, grad_value])
    embed_rows, qkv_rows = (
        lax.all_gather(embed_weight, "blk", axis=1, tiled=True),
        lax.all_gather(qkv_weight, "blk", axis=1, tiled=True),
    )
    partial_grad = jnp.einsum(
        "ste,sde->td", stacked_grads, qkv_rows, preferred_element_type=jnp.float32
    )
    grad_tokens = slab_total(partial_grad).astype(jnp.bfloat16)
    patch_grad = jnp.einsum(
        "td,pfd->tpf", grad_tokens, embed_rows, preferred_element_type=jnp.float32
    ).astype(jnp.bfloat16)
    grid_grad = patch_grad.reshape(y_blocks, z_blocks, x_local, PY, PZ, channels).transpose(
        2, 0, 3, 1, 4, 5
    )
    grid_grad = grid_grad.reshape(x_local, y_cells, z_total, channels)
    grid_grad = lax.all_to_all(grid_grad, "zslab", split_axis=2, concat_axis=0, tiled=True)
    for layer_num in reversed(range(LAYERS)):
        conv_out = conv_outs[layer_num]
        sigma = jax.nn.sigmoid(conv_out)
        slope_grad = (
            gate_mask * sigma * (1.0 + conv_out * (1.0 - sigma)) * grid_grad.astype(jnp.float32)
        ).astype(jnp.bfloat16)
        flipped = (
            conv_weight[layer_num]
            .reshape(27, channels, channels)
            .transpose(0, 2, 1)
            .reshape(27 * channels, channels)
        )
        backward = apply_offsets(
            with_rim(slope_grad), flipped, dilation[layer_num], -1, field.shape
        )
        grid_grad = (grid_grad.astype(jnp.float32) + backward).astype(jnp.bfloat16)
    return grid_grad


HALO = [(dz, dx) for dz in (-1, 0, 1) for dx in (-1, 0, 1) if (dz, dx) != (0, 0)]
ZS = 4
NB = 8
ND = ZS * NB
ZC, XC, YC, C = 4, 8, 16, 128
CELLS = ZC * XC * YC
F32 = jnp.float32
BF16 = jnp.bfloat16
CONTRACT_LAST = (((1,), (1,)), ((), ()))


def one_hot(target):
    rows = lax.broadcasted_iota(jnp.int32, (CELLS, 1), 0)
    cols = lax.broadcasted_iota(jnp.int32, (CELLS, CELLS), 1)
    return jnp.where(cols == target(rows), 1.0, 0.0).astype(F32).astype(BF16)


def bit(value, low, count):
    return (value >> low) & ((1 << count) - 1)


def cell_of_slot(r):
    zs, py, px_lo, pz, yp, zp_lo = (
        bit(r, 7, 2), bit(r, 4, 3), bit(r, 3, 1), bit(r, 2, 1), bit(r, 1, 1), bit(r, 0, 1)
    )
    return (zp_lo * 2 + pz) * 128 + (2 * zs + px_lo) * 16 + yp * 8 + py


def slot_of_cell(r):
    zp_lo, pz, zs, px_lo, yp, py = (
        bit(r, 8, 1), bit(r, 7, 1), bit(r, 5, 2), bit(r, 4, 1), bit(r, 3, 1), bit(r, 0, 3)
    )
    return (zs * 8 + py) * 16 + px_lo * 8 + pz * 4 + yp * 2 + zp_lo


def arrival_of_row(r):
    q, xp, yp, zs, zp_lo = bit(r, 7, 2), bit(r, 4, 3), bit(r, 3, 1), bit(r, 1, 2), bit(r, 0, 1)
    return (zs * 8 + xp) * 16 + q * 4 + yp * 2 + zp_lo


def row_of_arrival(r):
    zs, xp, q, yp, zp_lo = bit(r, 7, 2), bit(r, 4, 3), bit(r, 2, 2), bit(r, 1, 1), bit(r, 0, 1)
    return q * 128 + xp * 16 + yp * 8 + zs * 2 + zp_lo


def sigmoid(a):
    return 1.0 / (1.0 + jnp.exp(-a))


def span(step, size):
    if step == 0:
        return 2, 2, size
    return (size, 0, 2) if step == 1 else (2, size + 2, 2)


def kernel(
    dilation, field, mask, conv_hbm, embed_hbm, qkv_hbm, grad_hbm, out,
    pad_0, pad_1, pad_2, pad_3, gate_ref, orders, conv_w, embed, weights, grads, conv_outs,
    send_patch, got_patch, send_part, got_part, tokens,
    send_gt, got_gt, grad_tok, send_back, got_back,
    halo_send, halo_recv, load_sem, qkv_send, qkv_recv, fwd_send, fwd_recv,
    og_send, og_recv, all_send, all_recv, gt_send, gt_recv,
    send_row, got_row, row_send, row_recv,
):
    pads = (pad_0, pad_1, pad_2, pad_3)
    zs, b = lax.axis_index("zslab"), lax.axis_index("blk")
    me = zs * NB + b
    partner = b + 1 - 2 * lax.rem(b, 2)

    loads = [
        pltpu.make_async_copy(conv_hbm, conv_w, load_sem.at[0]),
        pltpu.make_async_copy(embed_hbm, embed, load_sem.at[1]),
        pltpu.make_async_copy(qkv_hbm, weights.at[b], load_sem.at[2]),
        pltpu.make_async_copy(grad_hbm, grads.at[b], load_sem.at[3]),
    ]
    for pad in pads:
        pad[...] = jnp.zeros_like(pad)
    loads += [
        pltpu.make_async_copy(field, pad_0.at[pl.ds(2, ZC), pl.ds(2, XC)], load_sem.at[4]),
        pltpu.make_async_copy(mask, gate_ref, load_sem.at[5]),
    ]
    barrier = pltpu.get_barrier_semaphore()

    @pl.loop(1, ND)
    def _(d):
        peer = lax.rem(me + d, ND)
        pl.semaphore_signal(
            barrier, inc=1, device_id=(peer // NB, lax.rem(peer, NB)),
            device_id_type=pl.DeviceIdType.MESH,
        )

    for load in loads[::-1]:
        load.start()
    for at, target in enumerate((cell_of_slot, arrival_of_row, row_of_arrival, slot_of_cell)):
        orders[at] = one_hot(target)
    loads[4].wait()
    pl.semaphore_wait(barrier, ND - 1)

    def remote(src, dst, send, recv, to):
        return pltpu.make_async_remote_copy(
            src_ref=src, dst_ref=dst, send_sem=send, recv_sem=recv,
            device_id=to, device_id_type=pl.DeviceIdType.MESH,
        )

    def halo_copy(n, d):
        dz, dx = HALO[d]
        z0, z1, zl = span(dz, ZC)
        x0, x1, xl = span(dx, XC)
        return remote(
            pads[n].at[pl.ds(z0, zl), pl.ds(x0, xl)], pads[n].at[pl.ds(z1, zl), pl.ds(x1, xl)],
            halo_send.at[n, d], halo_recv.at[n, d],
            (lax.rem(zs + dz + ZS, ZS), lax.rem(b + dx + NB, NB)),
        )

    def inside(dz, dx):
        return (zs + dz >= 0) & (zs + dz < ZS) & (b + dx >= 0) & (b + dx < NB)

    def send_halo(n):
        for d, (dz, dx) in enumerate(HALO):
            @pl.when(inside(dz, dx))
            def _():
                halo_copy(n, d).start()

    def wait_halo(n):
        for d, (dz, dx) in enumerate(HALO):
            @pl.when(inside(-dz, -dx))
            def _():
                halo_copy(n, d).wait_recv()

    def convolve(n, layer, direction):
        rx, ry, rz = dilation[layer, 0], dilation[layer, 1], dilation[layer, 2]
        places = [(i, k) for i in (-1, 0, 1) for k in (-1, 0, 1)]
        windows = jnp.concatenate(
            [
                pads[n][
                    pl.ds(2 + direction * k * rz, ZC), pl.ds(2 + direction * i * rx, XC)
                ].reshape(CELLS, C)
                for i, k in places
            ],
            axis=1,
        )

        def tap(i, j, k):
            at = (9 * (i + 1) + 3 * j + k + 1) * C
            return conv_w[layer, at:at + C, :]

        if direction == 1:
            matrix = jnp.concatenate(
                [jnp.concatenate([tap(i, j, k) for j in range(3)], axis=1) for i, k in places],
                axis=0,
            )
            summed = jnp.dot(windows, matrix, preferred_element_type=F32)
        else:
            matrix = jnp.concatenate(
                [jnp.concatenate([tap(i, j, k) for i, k in places], axis=1) for j in range(3)],
                axis=0,
            )
            summed = lax.dot_general(
                windows, matrix, CONTRACT_LAST, preferred_element_type=F32
            )
        y = lax.broadcasted_iota(jnp.int32, (CELLS, C), 0) & (YC - 1)

        def shifted(value, by):
            near = pltpu.roll(value, (-by) % CELLS, 0)
            far = pltpu.roll(value, (-2 * by) % CELLS, 0)
            source = y + by * ry
            return jnp.where((source >= 0) & (source < YC), jnp.where(ry == 1, near, far), 0.0)

        return (
            summed[:, C:2 * C]
            + shifted(summed[:, :C], -direction)
            + shifted(summed[:, 2 * C:], direction)
        )

    def all_copy(phase, d, src, dst):
        peer = lax.rem(me + d, ND)
        return remote(
            src, dst, all_send.at[phase], all_recv.at[phase],
            (lax.div(peer, NB), lax.rem(peer, NB)),
        )

    def all_bytes(phase, ref):
        part = ref.at[pl.ds(0, ND - 1)]
        return all_copy(phase, 1, part, part)

    def scatter(phase, sends, gets):
        @pl.loop(1, ND)
        def _(d):
            all_copy(phase, d, sends.at[lax.rem(me + d, ND)], gets.at[me]).start()

        gets[pl.ds(me, 1)] = sends[pl.ds(me, 1)]

    send_halo(0)

    def qkv_copy(d):
        return remote(
            qkv_hbm, weights.at[b], qkv_send.at[d], qkv_recv.at[d],
            (zs, partner if d == 0 else lax.rem(b + 2 * d, NB)),
        )

    def qkv_forward(d):
        held = weights.at[lax.rem(b - 2 * d + NB, NB)]
        return remote(held, held, fwd_send.at[d], fwd_recv.at[d], (zs, partner))

    def grad_copy(d):
        return remote(
            grad_hbm, grads.at[b], og_send.at[d], og_recv.at[d], (zs, lax.rem(b + d, NB))
        )

    for d in range(NB // 2):
        qkv_copy(d).start()
    for d in range(1, NB):
        grad_copy(d).start()

    loads[5].wait()
    gate = gate_ref[...]
    loads[0].wait()
    hidden = pad_0[2:6, 2:10].reshape(CELLS, C)
    for layer in range(LAYERS):
        if layer:
            pads[layer][2:6, 2:10] = hidden.reshape(ZC, XC, YC, C)
            send_halo(layer)
        wait_halo(layer)
        conv_out = convolve(layer, layer, 1)
        conv_outs[layer] = conv_out
        hidden = (hidden.astype(F32) + gate * (conv_out * sigmoid(conv_out))).astype(BF16)

    send_patch[...] = (
        jnp.dot(orders[0], hidden, preferred_element_type=F32)
        .astype(BF16).reshape(ND, 16, C)
    )
    scatter(0, send_patch, got_patch)
    for d in range(1, NB // 2):
        qkv_copy(d).wait_recv()
        qkv_forward(d).start()
    loads[1].wait()
    all_bytes(0, got_patch).wait_recv()
    ordered = jnp.dot(
        orders[1], got_patch[...].reshape(CELLS, C), preferred_element_type=F32
    ).astype(BF16)
    patches = jnp.concatenate([ordered[q * 128:(q + 1) * 128] for q in range(4)], axis=1)
    for part in range(ZS):
        columns = slice(part * 256, (part + 1) * 256)
        send_part[part * NB:(part + 1) * NB] = (
            jnp.dot(patches, embed[:, columns], preferred_element_type=F32)
            .astype(BF16).reshape(NB, 16, 256)
        )
    def slab_copy(phase, d, src, dst):
        return remote(
            src, dst, gt_send.at[phase, d], gt_recv.at[phase, d], (lax.rem(zs + d, ZS), b)
        )

    def row_copy(phase, d, src, dst):
        return remote(
            src, dst, row_send.at[phase, d], row_recv.at[phase, d], (zs, lax.rem(b + d, NB))
        )

    for d in range(1, ZS):
        slab_copy(
            2, d, send_part.at[pl.ds(lax.rem(zs + d, ZS) * NB, NB)],
            got_part.at[pl.ds(zs * NB, NB)],
        ).start()
    got_part[pl.ds(zs * NB, NB)] = send_part[pl.ds(zs * NB, NB)]
    for d in range(1, ZS):
        held = got_part.at[pl.ds(lax.rem(zs - d + ZS, ZS) * NB, NB)]
        slab_copy(2, d, held, held).wait_recv()
    send_row[...] = sum(
        got_part[part * NB:(part + 1) * NB].astype(F32) for part in range(ZS)
    ).astype(BF16)
    for d in range(1, NB):
        row_copy(0, d, send_row.at[lax.rem(b + d, NB)], got_row.at[b]).start()
    got_row[pl.ds(b, 1)] = send_row[pl.ds(b, 1)]
    for d in range(1, NB):
        held = got_row.at[lax.rem(b - d + NB, NB)]
        row_copy(0, d, held, held).wait_recv()
    tokens[pl.ds(me, 1)] = (
        jnp.sum(got_row[...].astype(F32), axis=0, keepdims=True).astype(BF16)
    )
    for d in range(1, NB):
        row_copy(1, d, tokens.at[me], tokens.at[me]).start()
    for d in range(1, NB):
        held = tokens.at[zs * NB + lax.rem(b - d + NB, NB)]
        row_copy(1, d, held, held).wait_recv()
    slab = tokens.at[pl.ds(zs * NB, NB)]
    for d in range(1, ZS):
        slab_copy(3, d, slab, slab).start()

    for load in loads[2:4]:
        load.wait()
    qkv_copy(0).wait_recv()
    for d in range(1, NB // 2):
        remote(
            qkv_hbm, weights.at[lax.rem(partner - 2 * d + NB, NB)],
            fwd_send.at[d], fwd_recv.at[d], (zs, partner),
        ).wait_recv()
    for d in range(1, NB):
        grad_copy(d).wait_recv()
    for d in range(1, ZS):
        held = tokens.at[pl.ds(lax.rem(zs - d + ZS, ZS) * NB, NB)]
        slab_copy(3, d, held, held).wait_recv()

    all_tokens = jnp.concatenate(
        [tokens[part * NB:(part + 1) * NB].reshape(128, 256) for part in range(ZS)], axis=1
    )
    projected = [
        jnp.dot(all_tokens, weights[:, s].reshape(1024, 256), preferred_element_type=F32)
        .astype(BF16)
        for s in range(3)
    ]
    grad_out = grads[...].reshape(128, 256)
    inv_root = HD ** (-0.5)
    pieces = []
    for head in range(2):
        columns = slice(head * HD, (head + 1) * HD)
        query, key, value = (array[:, columns] for array in projected)
        grad_h = grad_out[:, columns]
        scores = lax.dot_general(query, key, CONTRACT_LAST, preferred_element_type=F32) * inv_root
        expo = jnp.exp(scores - jnp.max(scores, axis=1, keepdims=True))
        probs = expo / jnp.sum(expo, axis=1, keepdims=True)
        probs_b = probs.astype(BF16)
        attended = jnp.dot(probs_b, value, preferred_element_type=F32)
        row_delta = jnp.sum(grad_h.astype(F32) * attended, axis=1, keepdims=True)
        score_grad = lax.dot_general(grad_h, value, CONTRACT_LAST, preferred_element_type=F32)
        dscore = probs * (score_grad - row_delta) * inv_root
        dscore_t = dscore.T.astype(BF16)
        probs_t = probs.T.astype(BF16)
        pieces.append((
            jnp.dot(dscore.astype(BF16), key, preferred_element_type=F32).astype(BF16),
            jnp.dot(dscore_t, query, preferred_element_type=F32).astype(BF16),
            jnp.dot(probs_t, grad_h, preferred_element_type=F32).astype(BF16),
        ))
    stacked = [jnp.concatenate([piece[s] for piece in pieces], axis=1) for s in range(3)]
    for part in range(ZS):
        term = jnp.zeros((128, 256), F32)
        for s in range(3):
            rows = weights[part * 2:part * 2 + 2, s].reshape(256, 256)
            term += lax.dot_general(stacked[s], rows, CONTRACT_LAST, preferred_element_type=F32)
        send_gt[part] = term.astype(BF16)

    for d in range(1, ZS):
        slab_copy(0, d, send_gt.at[lax.rem(zs + d, ZS)], got_gt.at[zs]).start()
    got_gt[pl.ds(zs, 1)] = send_gt[pl.ds(zs, 1)]
    for d in range(1, ZS):
        slab_copy(
            0, d, send_gt.at[lax.rem(zs + d, ZS)], got_gt.at[lax.rem(zs - d + ZS, ZS)]
        ).wait_recv()
    grad_tok[pl.ds(zs, 1)] = (
        jnp.sum(got_gt[...].astype(F32), axis=0, keepdims=True).astype(BF16)
    )
    for d in range(1, ZS):
        slab_copy(1, d, grad_tok.at[zs], grad_tok.at[zs]).start()
    for d in range(1, ZS):
        held = grad_tok.at[lax.rem(zs - d + ZS, ZS)]
        slab_copy(1, d, held, held).wait_recv()
    all_grad = jnp.concatenate([grad_tok[part] for part in range(ZS)], axis=1)
    patch_grad = jnp.concatenate(
        [
            lax.dot_general(
                all_grad, embed[q * 128:(q + 1) * 128, :], CONTRACT_LAST,
                preferred_element_type=F32,
            ).astype(BF16)
            for q in range(4)
        ],
        axis=0,
    )
    send_back[...] = (
        jnp.dot(orders[2], patch_grad, preferred_element_type=F32)
        .astype(BF16).reshape(ND, 16, C)
    )
    scatter(3, send_back, got_back)
    all_bytes(3, got_back).wait_recv()
    grid_grad = jnp.dot(orders[3], got_back[...].reshape(CELLS, C), preferred_element_type=F32)
    for layer in reversed(range(LAYERS)):
        conv_out = conv_outs[layer]
        sigma = sigmoid(conv_out)
        slope = gate * sigma * (1.0 + conv_out * (1.0 - sigma)) * grid_grad
        n = 2 * LAYERS - 1 - layer
        pads[n][2:6, 2:10] = slope.astype(BF16).reshape(ZC, XC, YC, C)
        send_halo(n)
        wait_halo(n)
        grid_grad = (grid_grad + convolve(n, layer, -1)).astype(BF16).astype(F32)
    out[...] = grid_grad.astype(BF16).reshape(ZC, XC, YC, C)

    for n in range(2 * LAYERS):
        for d, (dz, dx) in enumerate(HALO):
            @pl.when(inside(dz, dx))
            def _():
                halo_copy(n, d).wait_send()
    for d in range(NB // 2):
        qkv_copy(d).wait_send()
        if d:
            qkv_forward(d).wait_send()
    for d in range(1, NB):
        grad_copy(d).wait_send()
    for phase, ref in ((0, send_patch), (3, send_back)):
        all_bytes(phase, ref).wait_send()
    for phase in range(2):
        for d in range(1, NB):
            row_copy(phase, d, send_row.at[0], got_row.at[0]).wait_send()
    for d in range(1, ZS):
        slab_copy(2, d, slab, slab).wait_send()
        slab_copy(3, d, slab, slab).wait_send()
    for phase in range(2):
        for d in range(1, ZS):
            slab_copy(phase, d, send_gt.at[0], got_gt.at[0]).wait_send()


def fused(field, fracture_mask, dilation, conv_weight, embed_weight, qkv_weight, out_grad):
    cells = field.transpose(2, 0, 1, 3)
    gate = jnp.broadcast_to(
        fracture_mask.transpose(2, 0, 1).reshape(CELLS, 1).astype(F32), (CELLS, C)
    )
    vmem = pl.BlockSpec(memory_space=pltpu.VMEM)
    hbm = pl.BlockSpec(memory_space=pltpu.HBM)
    dma = pltpu.SemaphoreType.DMA
    result = pl.pallas_call(
        kernel,
        out_shape=jax.ShapeDtypeStruct(cells.shape, BF16),
        in_specs=[pl.BlockSpec(memory_space=pltpu.SMEM)] + [hbm] * 6,
        out_specs=vmem,
        scratch_shapes=[
            *[pltpu.VMEM((ZC + 4, XC + 4, YC, C), BF16)] * (2 * LAYERS),
            pltpu.VMEM((CELLS, C), F32),
            pltpu.VMEM((4, CELLS, CELLS), BF16),
            pltpu.VMEM(conv_weight.shape, BF16),
            pltpu.VMEM((512, 1024), BF16),
            pltpu.VMEM((NB, 3, 128, 256), BF16),
            pltpu.VMEM((NB, 16, 256), BF16),
            pltpu.VMEM((LAYERS, CELLS, C), F32),
            pltpu.VMEM((ND, 16, C), BF16),
            pltpu.VMEM((ND, 16, C), BF16),
            pltpu.VMEM((ND, 16, 256), BF16),
            pltpu.VMEM((ND, 16, 256), BF16),
            pltpu.VMEM((ND, 16, 256), BF16),
            pltpu.VMEM((ZS, 128, 256), BF16),
            pltpu.VMEM((ZS, 128, 256), BF16),
            pltpu.VMEM((ZS, 128, 256), BF16),
            pltpu.VMEM((ND, 16, C), BF16),
            pltpu.VMEM((ND, 16, C), BF16),
            dma((2 * LAYERS, 8)),
            dma((2 * LAYERS, 8)),
            dma((6,)),
            dma((NB // 2,)),
            dma((NB // 2,)),
            dma((NB // 2,)),
            dma((NB // 2,)),
            dma((NB,)),
            dma((NB,)),
            dma((4,)),
            dma((4,)),
            dma((4, ZS)),
            dma((4, ZS)),
            pltpu.VMEM((NB, 16, 256), BF16),
            pltpu.VMEM((NB, 16, 256), BF16),
            dma((2, NB)),
            dma((2, NB)),
        ],
        compiler_params=pltpu.CompilerParams(
            collective_id=0, has_side_effects=True
        ),
    )(
        dilation, cells, gate, conv_weight, embed_weight.reshape(512, 1024), qkv_weight, out_grad
    )
    return result.transpose(1, 2, 0, 3)


def block(*arrays):
    field, embed_weight, qkv_weight, out_grad = (arrays[0], arrays[4], arrays[5], arrays[6])
    fits = (
        (lax.axis_size("zslab"), lax.axis_size("blk")) == (ZS, NB)
        and field.shape == (XC, YC, ZC, C)
        and embed_weight.shape == (2, 256, 1024)
        and qkv_weight.shape == (3, 128, 256)
        and out_grad.shape == (16, 256)
    )
    return fused(*arrays) if fits else local(*arrays)


def solution(mesh):
    return jax.shard_map(
        block,
        mesh=mesh,
        in_specs=(
            P("blk", None, "zslab", None),
            P("blk", None, "zslab"),
            P(),
            P(),
            P("zslab", "blk", None),
            P(None, "blk", "zslab"),
            P("blk", "zslab"),
        ),
        out_specs=P("blk", None, "zslab", None),
        check_vma=False,
    )
```
